32 devices in a mesh: frames: 2 (over y), row: 4 (over x, core), col: 4 (over z).
Axes of the slice: x: 2, y: 2, z: 4, core: 2. Of those that a mesh axis runs over, the one named last changes fastest.
Arguments:
- mask_pixels: int32 [2048, 2048], P(('frames', 'row'), 'col'), parts along dimension 0, may hold values 0 or 1
- across_taps: bfloat16 [12, 2, 33], replicated, may hold values from -1 to 1
- down_taps: bfloat16 [12, 2, 33], replicated, may hold values from -1 to 1
- kernel_weights: float32 [12], replicated, may hold values from 0.05 to 0.5
- library: bfloat16 [32, 64, 128], P('col'), may hold values from 0 to 4
- cell_ids: int32 [8, 4, 8], P(('frames', 'row'), 'col'), parts along dimension 0, may hold values from 0 to 31, as said below
- cell_slots: int32 [8, 4, 8], P(('frames', 'row'), 'col'), parts along dimension 0, may hold values from 0 to 15, as said below
- cell_count: int32 [8, 4], P(('frames', 'row'), 'col'), parts along dimension 0, may hold values from 2 to 8
Outputs:
- resist: float32 [2048, 2048], P(('frames', 'row'), 'col'), parts along dimension 0
The draws below stay inside these ranges and needn't reach their ends.
There are 2 independent parts, one for each index of `frames`. The reference program is written for one: setup_inputs(seed, part) draws one part's arguments, and reference() takes and returns one part's arrays. A program takes and returns all parts, laid end to end along the dimension named above; an argument that names none is the same for every part. Nothing has to cross between parts.
Inputs may be any that keep to these rules, and one draw needn't show every extreme that they name: `cell_ids`: among the 8 entries of a tile's list, at most 2 name cells of one block of 8 consecutive ids (k * 8 to k * 8 + 7), and the first two entries name cells of one such block. `cell_slots`: the slots of a tile's list are distinct.
All inputs are finite; a program needn't handle non-finite values. No bound on the sum of `mask_pixels` on one device may be relied on, other than what follows from the above.
Results may differ from the reference program's by a relative error of at most 0.00045.
Values may be sent and summed in bfloat16 or wider, within the bound.
A program may use at most 64 MiB of HBM per device.

```python
import math
import jax
import jax.numpy as jnp
from jax import lax

KERNELS = 12
XHALF = 16
BLUR_HALF = 8
CELL_R = 64
CELL_C = 128
CELL_DEV = 8
ROWS = 1024
COLS = 2048
NCELL = 32
SLOTS = 16
MAXI = 8
N_ROW = 4
N_COL = 4


def draw_library(key, part):
    key_list = jax.random.split(jax.random.fold_in(key, 5003), 2)
    block_shape = (NCELL, CELL_R // 4, CELL_C // 4)
    theta = jax.random.uniform(key_list[0], block_shape, jnp.float32, 0.0, 6.283185307)
    level = 2.0 + 1.96 * jnp.tanh(4.0 * jnp.sin(theta))
    factor = jax.random.uniform(key_list[1], (NCELL, CELL_R, CELL_C), jnp.float32, 0.8, 1.0)
    level = jnp.repeat(jnp.repeat(level, 4, axis=1), 4, axis=2)
    return (level * factor).astype(jnp.bfloat16)


def instance_tables(key):
    key_list = jax.random.split(jax.random.fold_in(key, 7001), 12)
    tile_grid = (N_ROW, N_COL)
    band_owner = jax.random.randint(key_list[0], (N_ROW, 1), 0, N_COL)
    tile_owner = jax.random.randint(key_list[1], tile_grid, 0, N_COL)
    band_flag = jax.random.randint(key_list[2], (N_ROW, 1), 0, 2)
    forced_band = jax.random.randint(key_list[3], (), 0, N_ROW)
    band_flag = jnp.where(jnp.arange(N_ROW, dtype=jnp.int32)[:, None] == forced_band, 1, band_flag)
    first_owner = jnp.where(band_flag == 1, band_owner, tile_owner)
    owner_iota = jnp.arange(N_COL, dtype=jnp.int32)
    owner_score = jax.random.randint(key_list[4], tile_grid + (N_COL,), 0, 1 << 20) * N_COL + owner_iota
    owner_score = jnp.where(owner_iota == first_owner[..., None], -1, owner_score)
    ranked = jnp.argsort(owner_score, axis=-1).astype(jnp.int32)
    others = jnp.concatenate([ranked[..., 1:], ranked[..., 1:]], axis=-1)
    spare = 2 * N_COL - 2
    shuffle_score = jax.random.randint(key_list[5], tile_grid + (spare,), 0, 1 << 20) * (2 * N_COL) + jnp.arange(spare, dtype=jnp.int32)
    shuffle_order = jnp.argsort(shuffle_score, axis=-1)
    others = jnp.take_along_axis(others, shuffle_order, axis=-1)
    owners = jnp.concatenate([ranked[..., :1], ranked[..., :1], others], axis=-1)[..., :MAXI]
    local_index = jax.random.randint(key_list[6], tile_grid + (MAXI,), 0, CELL_DEV)
    cell_ids = owners * CELL_DEV + local_index
    slot_score = jax.random.randint(key_list[7], tile_grid + (SLOTS,), 0, 1 << 20) * SLOTS + jnp.arange(SLOTS, dtype=jnp.int32)
    cell_slots = jnp.argsort(slot_score, axis=-1)[..., :MAXI]
    first_draw = jax.random.randint(key_list[8], tile_grid, 0, MAXI)
    second_draw = jax.random.randint(key_list[9], tile_grid, 0, MAXI)
    cell_count = MAXI - first_draw * second_draw // MAXI
    tile_iota = jnp.arange(N_ROW * N_COL, dtype=jnp.int32).reshape(tile_grid)
    full_tile = jax.random.randint(key_list[10], (), 0, N_ROW * N_COL)
    short_tile = (full_tile + 1 + jax.random.randint(key_list[11], (), 0, N_ROW * N_COL - 1)) % (N_ROW * N_COL)
    cell_count = jnp.where(tile_iota == full_tile, MAXI, cell_count)
    cell_count = jnp.where(tile_iota == short_tile, 2, cell_count)
    return (cell_ids.astype(jnp.int32), cell_slots.astype(jnp.int32), cell_count.astype(jnp.int32))


def draw_cell_ids(key, part):
    return instance_tables(key)[0]


def draw_cell_slots(key, part):
    return instance_tables(key)[1]


def draw_cell_count(key, part):
    return instance_tables(key)[2]


def set_ends(values, key, least, largest):
    shape = values.shape
    place = [jax.random.randint(jax.random.fold_in(key, axis), (), 0, shape[axis]) for axis in range(len(shape))]
    values = values.at[tuple(place)].set(least)
    longest = shape.index(max(shape))
    place[longest] = (place[longest] + 1) % shape[longest]
    return values.at[tuple(place)].set(largest)


def scatter_about(stream_key, extent, width, reach, kind=jnp.bfloat16):
    return jnp.clip(width * jax.random.normal(stream_key, extent, jnp.float32), -reach, reach).astype(kind)


def setup_inputs(seed: int = 0, part: int = 0) -> dict:
    streams_of = jax.random.split(jax.random.key(seed), 9)
    part_keys = jax.random.split(jax.random.fold_in(streams_of[8], part), 9)
    return {
        "mask_pixels": set_ends((jax.random.randint(part_keys[0], (ROWS, COLS), 0, 2) < 1).astype(jnp.int32), jax.random.fold_in(part_keys[0], 1), 0, 1),
        "across_taps": scatter_about(streams_of[1], (KERNELS, 2, 2 * XHALF + 1), (2 * XHALF + 1) ** -0.5, 1.0),
        "down_taps": scatter_about(streams_of[2], (KERNELS, 2, 2 * XHALF + 1), (2 * XHALF + 1) ** -0.5, 1.0),
        "kernel_weights": jnp.clip(jnp.exp(jax.random.uniform(streams_of[3], (KERNELS,), jnp.float32, math.log(0.05), math.log(0.5))), 0.05, 0.5),
        "library": draw_library(jax.random.fold_in(streams_of[8], 71), part),
        "cell_ids": draw_cell_ids(jax.random.fold_in(jax.random.fold_in(streams_of[8], part), 71), part),
        "cell_slots": draw_cell_slots(jax.random.fold_in(jax.random.fold_in(streams_of[8], part), 71), part),
        "cell_count": draw_cell_count(jax.random.fold_in(jax.random.fold_in(streams_of[8], part), 71), part),
    }


BLUR_SIGMA = 4.0


def band_matrix(tap_values, half_width):
    window = 128 + 2 * half_width
    grid_shape = (window, 128, 2 * half_width + 1)
    in_index = lax.broadcasted_iota(jnp.int32, grid_shape, 0)
    out_index = lax.broadcasted_iota(jnp.int32, grid_shape, 1)
    lag_index = lax.broadcasted_iota(jnp.int32, grid_shape, 2)
    picker = (in_index - out_index == lag_index).astype(jnp.float32)
    return jnp.einsum("...t,ijt->...ij", tap_values.astype(jnp.float32), picker, precision=lax.Precision.HIGHEST)


def blur_taps(half_width):
    offsets = lax.broadcasted_iota(jnp.int32, (2 * half_width + 1,), 0).astype(jnp.float32) - half_width
    weights = jnp.exp(-offsets * offsets / (2.0 * BLUR_SIGMA * BLUR_SIGMA))
    return weights / jnp.sum(weights)


def windows_last(padded, half_width):
    length = padded.shape[-1] - 2 * half_width
    blocks = length // 128
    pad_spec = [(0, 0)] * (padded.ndim - 1) + [(0, 128 - 2 * half_width)]
    spread = jnp.pad(padded, pad_spec).reshape(padded.shape[:-1] + (blocks + 1, 128))
    return jnp.concatenate([spread[..., :blocks, :], spread[..., 1:, :2 * half_width]], axis=-1)


def windows_rows(padded, half_width):
    length = padded.shape[-2] - 2 * half_width
    blocks = length // 128
    pad_spec = [(0, 0)] * (padded.ndim - 2) + [(0, 128 - 2 * half_width), (0, 0)]
    spread = jnp.pad(padded, pad_spec).reshape(padded.shape[:-2] + (blocks + 1, 128, padded.shape[-1]))
    return jnp.concatenate([spread[..., :blocks, :, :], spread[..., 1:, :2 * half_width, :]], axis=-2)


def blur_straight(extended, blur_mat, half_width):
    sideways = jnp.einsum("rbi,ij->rbj", windows_last(extended, half_width), blur_mat, precision=lax.Precision.HIGHEST)
    sideways = sideways.reshape(extended.shape[0], -1)
    downward = jnp.einsum("biw,ij->bjw", windows_rows(sideways, half_width), blur_mat, precision=lax.Precision.HIGHEST)
    return downward.reshape(-1, sideways.shape[1])


def reference(mask_pixels, across_taps, down_taps, kernel_weights, library, cell_ids, cell_slots, cell_count):
    half_width = (across_taps.shape[-1] - 1) // 2
    frame_rows, frame_cols = mask_pixels.shape
    pixels = mask_pixels.astype(jnp.float32)
    padded_mask = jnp.pad(pixels, ((0, 0), (half_width, half_width)))
    mask_windows = windows_last(padded_mask, half_width)
    first_mats = band_matrix(across_taps, half_width)
    second_mats = band_matrix(down_taps, half_width)
    flat_image = jnp.zeros((frame_rows, frame_cols), jnp.float32)
    for kernel in range(across_taps.shape[0]):
        pass_one = jnp.einsum("rbi,pij->prbj", mask_windows, first_mats[kernel], precision=lax.Precision.HIGHEST)
        pass_one = pass_one.reshape(2, frame_rows, frame_cols)
        pass_one = lax.optimization_barrier(pass_one.astype(jnp.bfloat16)).astype(jnp.float32)
        extended = jnp.pad(pass_one, ((0, 0), (half_width, half_width), (0, 0)))
        pass_two = jnp.einsum("pbiw,pij->pbjw", windows_rows(extended, half_width), second_mats[kernel], precision=lax.Precision.HIGHEST)
        pass_two = pass_two.reshape(2, frame_rows, frame_cols)
        flat_image = flat_image + kernel_weights[kernel] * jnp.sum(pass_two * pass_two, axis=0)
    tiles_r, tiles_c, entries = cell_ids.shape
    tile_rows = frame_rows // tiles_r
    tile_cols = frame_cols // tiles_c
    cell_rows, cell_cols = library.shape[1], library.shape[2]
    slot_rows = tile_rows // cell_rows
    slot_cols = tile_cols // cell_cols
    is_live = lax.broadcasted_iota(jnp.int32, (tiles_r, tiles_c, entries), 2) < cell_count[:, :, None]
    slot_hit = (cell_slots[..., None] == lax.broadcasted_iota(jnp.int32, (1, 1, 1, slot_rows * slot_cols), 3)) & is_live[..., None]
    slot_hit = slot_hit.astype(jnp.float32).reshape(tiles_r, tiles_c, entries, slot_rows, slot_cols)
    images = jnp.take(library, cell_ids, axis=0).astype(jnp.float32)
    placed = jnp.einsum("rcmab,rcmpq->rapcbq", slot_hit, images, precision=lax.Precision.HIGHEST)
    placed = placed.reshape(frame_rows, frame_cols)
    intensity = flat_image + placed
    blur_mat = band_matrix(blur_taps(BLUR_HALF), BLUR_HALF)
    extended = jnp.pad(intensity, ((BLUR_HALF, BLUR_HALF), (BLUR_HALF, BLUR_HALF)))
    return blur_straight(extended, blur_mat, BLUR_HALF)
```

```python
import functools
import math

import jax
import jax.numpy as jnp
from jax import lax
from jax.experimental import pallas as pl
from jax.experimental.pallas import tpu as pltpu
from jax.sharding import PartitionSpec as P

BLUR = 8
SIGMA = 4.0
GAUSS_SUM = sum(math.exp(-(t * t) / (2.0 * SIGMA * SIGMA)) for t in range(-BLUR, BLUR + 1))
MESH = pl.DeviceIdType.MESH
F32 = jnp.float32
BF16 = jnp.bfloat16
LANES = 128
AROUND = [(i, j) for i in (-1, 0, 1) for j in (-1, 0, 1)]
HERE = 4
RIM_ROWS = 32


def gauss_band(shape, in_dim):
    step = lax.broadcasted_iota(jnp.int32, shape, in_dim) - lax.broadcasted_iota(
        jnp.int32, shape, 1 - in_dim
    )
    lag = step.astype(F32) - BLUR
    value = jnp.exp(-lag * lag / (2.0 * SIGMA * SIGMA)) * (1.0 / GAUSS_SUM)
    value = jnp.where((step >= 0) & (step <= 2 * BLUR), value, 0.0)
    high = value.astype(BF16)
    return high, (value - high.astype(F32)).astype(BF16)


def dot(a, b):
    return jnp.dot(a, b, preferred_element_type=F32)


def kernel(
    half,
    n_row,
    n_col,
    mask_ref,
    across_ref,
    down_ref,
    weights_ref,
    library_ref,
    ids_ref,
    slots_ref,
    count_ref,
    out_ref,
    own,
    up_down,
    left_right,
    corners,
    mask_ext,
    tap_rows,
    down_mats,
    across_mats,
    first,
    total,
    high,
    low,
    cells,
    table,
    tables,
    tables_s,
    mask_send,
    mask_recv,
    table_send,
    table_recv,
    cell_send,
    cell_recv,
    table_sem,
):
    rows, cols = mask_ref.shape
    kernels = across_ref.shape[0]
    taps = 2 * half + 1
    rim = half + BLUR
    wide = own.shape[1]
    out_rows = rows + 2 * BLUR
    blocks = cols // LANES
    n_cells, cell_rows, _ = library_ref.shape
    slot_rows = rows // cell_rows
    row, col = lax.axis_index("row"), lax.axis_index("col")

    def exists(dr, dc):
        ok = None
        for here, step, count in ((row, dr, n_row), (col, dc, n_col)):
            if step < 0:
                one = here >= -step
            elif step > 0:
                one = here < count - step
            else:
                continue
            ok = one if ok is None else ok & one
        return ok

    def device(dr, dc):
        return {"row": row + dr, "col": col + dc}

    peers = [(0, j) for j in range(-(n_col - 1), n_col) if j != 0]
    near = [o for o in AROUND if o != (0, 0)]
    partners = near + [o for o in peers if abs(o[1]) > 1]

    barrier = pltpu.get_barrier_semaphore()
    for o in partners:

        @pl.when(exists(*o))
        def _():
            pl.semaphore_signal(barrier, inc=1, device_id=device(*o), device_id_type=MESH)

    pixels = mask_ref[...].astype(F32)
    pixels = jnp.concatenate([pixels, jnp.zeros((rows, wide - cols), F32)], axis=1)
    own[...] = pltpu.roll(pixels, rim, 1).astype(BF16)
    entries = ids_ref.shape[-1]
    at_slot = lax.broadcasted_iota(jnp.int32, table.shape, 0)
    value = jnp.zeros(table.shape, jnp.int32)
    for n in range(entries):
        entry = jnp.where(n < count_ref[0, 0], ids_ref[0, 0, n] + 1, 0)
        value = value + jnp.where(at_slot == slots_ref[0, 0, n], entry, 0)
    table[...] = value

    pl.semaphore_wait(barrier, sum(jnp.where(exists(*o), 1, 0) for o in partners))

    def mask_copy(dr, dc):
        row_part = {-1: pl.ds(0, RIM_ROWS), 0: pl.ds(0, rows), 1: pl.ds(rows - RIM_ROWS, RIM_ROWS)}
        col_part = {-1: pl.ds(0, LANES), 0: pl.ds(0, wide), 1: pl.ds(cols, LANES)}
        slot = AROUND.index((-dr, -dc))
        if dc == 0:
            target = up_down.at[(1 - dr) // 2]
        elif dr == 0:
            target = left_right.at[(1 - dc) // 2]
        else:
            target = corners.at[(1 - dr) // 2 * 2 + (1 - dc) // 2]
        return pltpu.make_async_remote_copy(
            src_ref=own.at[row_part[dr], col_part[dc]],
            dst_ref=target,
            send_sem=mask_send.at[slot],
            recv_sem=mask_recv.at[slot],
            device_id=device(dr, dc),
            device_id_type=MESH,
        )

    def table_copy(dr, dc):
        slot = AROUND.index((-dr, -dc))
        return pltpu.make_async_remote_copy(
            src_ref=table,
            dst_ref=tables.at[slot],
            send_sem=table_send.at[slot],
            recv_sem=table_recv.at[slot],
            device_id=device(dr, dc),
            device_id_type=MESH,
        )

    def cell_copy(dc, owner):
        return pltpu.make_async_remote_copy(
            src_ref=library_ref,
            dst_ref=cells.at[pl.ds(owner * n_cells, n_cells)],
            send_sem=cell_send.at[dc + n_col],
            recv_sem=cell_recv.at[dc + n_col],
            device_id=device(0, dc),
            device_id_type=MESH,
        )

    for o in near:

        @pl.when(exists(*o))
        def _():
            mask_copy(*o).start()

    for o in near:

        @pl.when(exists(*o))
        def _():
            table_copy(*o).start()

    for _, dc in sorted(peers, key=lambda o: abs(o[1])):

        @pl.when(exists(0, dc))
        def _():
            cell_copy(dc, col).start()

    tap_rows[...] = jnp.zeros_like(tap_rows)
    for k in range(kernels):
        tap_rows[0, 2 * k : 2 * k + 2, :taps] = down_ref[k].astype(F32)
        tap_rows[1, 2 * k : 2 * k + 2, :taps] = across_ref[k].astype(F32)
    pick = lax.broadcasted_iota(jnp.int32, (LANES, 2 * LANES), 0)
    lane = lax.broadcasted_iota(jnp.int32, (LANES, 2 * LANES), 1)
    shift = RIM_ROWS - rim
    forward = (lane == pick + shift).astype(BF16)
    backward = ((lane + pick) % (2 * LANES) == 0).astype(BF16)
    base_down = dot(tap_rows[0, :, :LANES].astype(BF16), forward)
    base_across = dot(tap_rows[1, :, :LANES].astype(BF16), backward)
    tap_rows[0] = base_down
    tap_rows[1] = base_across
    band_rows = down_mats.shape[1]

    def build(i, carry):
        one = jnp.broadcast_to(tap_rows[0, pl.ds(i, 1), :], (band_rows, 2 * LANES))
        down_mats[i] = pltpu.roll(one, 0, 1, stride=1, stride_axis=0).astype(BF16)
        one = jnp.broadcast_to(tap_rows[1, pl.ds(i, 1), :], (2 * LANES, 2 * LANES))
        across_mats[i] = pltpu.roll(one, 0, 1, stride=1, stride_axis=0).astype(BF16)
        return carry

    lax.fori_loop(0, 2 * kernels, build, 0)

    total[...] = jnp.zeros_like(total)
    mask_ext[rows + 2 * RIM_ROWS :, :] = jnp.zeros_like(mask_ext[rows + 2 * RIM_ROWS :, :])
    cells[pl.ds(col * n_cells, n_cells)] = library_ref[...]
    tables[HERE] = table[...]

    for o in near:
        slot = AROUND.index(o)

        @pl.when(exists(*o))
        def _():
            table_copy(-o[0], -o[1]).wait_recv()

        @pl.when(jnp.logical_not(exists(*o)))
        def _():
            tables[slot] = jnp.zeros(tables.shape[1:], jnp.int32)

    to_scalar = pltpu.make_async_copy(tables, tables_s, table_sem)
    to_scalar.start()

    for o in near:
        dr, dc = o

        @pl.when(exists(*o))
        def _():
            mask_copy(-dr, -dc).wait_recv()

        @pl.when(jnp.logical_not(exists(*o)))
        def _():
            if dc == 0:
                up_down[(1 + dr) // 2] = jnp.zeros(up_down.shape[1:], BF16)
            elif dr == 0:
                left_right[(1 + dc) // 2] = jnp.zeros(left_right.shape[1:], BF16)
            else:
                corners[(1 + dr) // 2 * 2 + (1 + dc) // 2] = jnp.zeros(corners.shape[1:], BF16)

    def extend(start, body, left, right):
        count = body.shape[0]
        part = pl.ds(start, count)
        near_edge = lax.broadcasted_iota(jnp.int32, (count, LANES), 1) < 2 * rim
        mask_ext[part, 0:LANES] = body[:, 0:LANES] + left
        mask_ext[part, LANES:cols] = body[:, LANES:cols]
        mask_ext[part, cols:wide] = body[:, cols:wide] + jnp.where(
            near_edge, right.astype(F32), 0.0
        ).astype(BF16)

    extend(0, up_down[0], corners[0], corners[1])
    extend(RIM_ROWS, own[...], left_right[0], left_right[1])
    extend(RIM_ROWS + rows, up_down[1], corners[2], corners[3])

    rest = out_rows - band_rows

    def down_pass(k, carry):
        lhs = down_mats[pl.ds(2 * k, 2)].reshape(2 * band_rows, 2 * LANES)
        got = dot(lhs, mask_ext[0 : 2 * LANES, :]).astype(BF16)
        first[2 * k, 0:band_rows] = got[:band_rows]
        first[2 * k + 1, 0:band_rows] = got[band_rows:]
        got = dot(lhs, mask_ext[band_rows : band_rows + 2 * LANES, :]).astype(BF16)
        first[2 * k, band_rows:] = got[:rest]
        first[2 * k + 1, band_rows:] = got[band_rows : band_rows + rest]
        return carry

    lax.fori_loop(0, kernels, down_pass, 0)

    def across_pass(k, carry):
        weight = weights_ref[k]
        for w in range(blocks):
            start = w * LANES
            stop = start + LANES if w < blocks - 1 else wide
            sums = None
            for p in range(2):
                got = dot(
                    first[2 * k + p, :, start : start + 2 * LANES],
                    across_mats[2 * k + p, :, : stop - start],
                )
                sums = got * got if sums is None else sums + got * got
            total[:, start:stop] = total[:, start:stop] + weight * sums
        return carry

    lax.fori_loop(0, kernels, across_pass, 0)

    for _, dc in peers:

        @pl.when(exists(0, dc))
        def _():
            cell_copy(-dc, col + dc).wait_recv()

    to_scalar.wait()

    def image(where, slot, part):
        entry = tables_s[where, slot, 0]
        scale = jnp.where(entry > 0, 1.0, 0.0)
        index = jnp.minimum(jnp.maximum(entry - 1, 0), cells.shape[0] - 1)
        return cells[index, part, :].astype(F32) * scale

    def place(start, dr, slot_row, part, keep):
        middle = AROUND.index((dr, 0))
        pieces = [image(middle, slot_row * blocks + b, part) for b in range(blocks)]
        before = image(middle - 1, slot_row * blocks + blocks - 1, part)
        after = image(middle + 1, slot_row * blocks, part)
        first_half = lax.broadcasted_iota(jnp.int32, before.shape, 1) < LANES // 2
        pieces.append(jnp.where(first_half, after, before))
        band = pltpu.roll(jnp.concatenate(pieces, axis=1), BLUR, 1)[keep]
        total[start : start + band.shape[0], :] = total[start : start + band.shape[0], :] + band

    place(0, -1, slot_rows - 1, pl.ds(cell_rows - 16, 16), slice(8, 16))
    for a in range(slot_rows):
        place(BLUR + a * cell_rows, 0, a, pl.ds(0, cell_rows), slice(0, cell_rows))
    place(BLUR + rows, 1, 0, pl.ds(0, 16), slice(0, 8))

    row_from = jnp.where(row == 0, BLUR, 0)
    row_to = jnp.where(row == n_row - 1, BLUR + rows, out_rows)
    col_from = jnp.where(col == 0, BLUR, 0)
    col_to = jnp.where(col == n_col - 1, BLUR + cols, cols + 2 * BLUR)
    at_row = lax.broadcasted_iota(jnp.int32, (out_rows, wide), 0)
    at_col = lax.broadcasted_iota(jnp.int32, (out_rows, wide), 1)
    inside = (at_row >= row_from) & (at_row < row_to) & (at_col >= col_from) & (at_col < col_to)
    value = jnp.where(inside, total[...], 0.0)
    top = value.astype(BF16)
    high[...] = top
    low[...] = (value - top.astype(F32)).astype(BF16)

    g_high, g_low = gauss_band((2 * LANES, LANES), 0)
    for w in range(blocks):
        here = slice(w * LANES, (w + 2) * LANES)
        got = dot(high[:, here], g_high) + dot(low[:, here], g_high) + dot(high[:, here], g_low)
        total[:, w * LANES : (w + 1) * LANES] = got
    value = total[:, :cols]
    top = value.astype(BF16)
    high[:, :cols] = top
    low[:, :cols] = (value - top.astype(F32)).astype(BF16)
    g_high, g_low = gauss_band((LANES, LANES + 2 * BLUR), 1)
    for r in range(rows // LANES):
        here = slice(r * LANES, (r + 1) * LANES + 2 * BLUR)
        out_ref[r * LANES : (r + 1) * LANES, :] = (
            dot(g_high, high[here, :cols])
            + dot(g_high, low[here, :cols])
            + dot(g_low, high[here, :cols])
        )

    for o in near:

        @pl.when(exists(*o))
        def _():
            mask_copy(*o).wait_send()
            table_copy(*o).wait_send()

    for _, dc in peers:

        @pl.when(exists(0, dc))
        def _():
            cell_copy(dc, col).wait_send()


def on_device(n_row, n_col, *args):
    mask_pixels, across_taps, _, _, library, cell_ids, _, _ = args
    rows, cols = mask_pixels.shape
    kernels = across_taps.shape[0]
    half = (across_taps.shape[-1] - 1) // 2
    wide = cols + LANES
    out_rows = rows + 2 * BLUR
    n_cells, cell_rows, cell_cols = library.shape
    n_slots = (rows // cell_rows) * (cols // cell_cols)
    band_rows = 144
    vmem = pl.BlockSpec(memory_space=pltpu.VMEM)
    smem = pl.BlockSpec(memory_space=pltpu.SMEM)
    dma = pltpu.SemaphoreType.DMA
    return pl.pallas_call(
        functools.partial(kernel, half, n_row, n_col),
        out_shape=jax.ShapeDtypeStruct((rows, cols), F32),
        in_specs=[vmem, vmem, vmem, smem, vmem, smem, smem, smem],
        out_specs=vmem,
        scratch_shapes=[
            pltpu.VMEM((rows, wide), BF16),
            pltpu.VMEM((2, RIM_ROWS, wide), BF16),
            pltpu.VMEM((2, rows, LANES), BF16),
            pltpu.VMEM((4, RIM_ROWS, LANES), BF16),
            pltpu.VMEM((band_rows + 2 * LANES, wide), BF16),
            pltpu.VMEM((2, 2 * kernels, 2 * LANES), F32),
            pltpu.VMEM((2 * kernels, band_rows, 2 * LANES), BF16),
            pltpu.VMEM((2 * kernels, 2 * LANES, 2 * LANES), BF16),
            pltpu.VMEM((2 * kernels, out_rows, wide), BF16),
            pltpu.VMEM((out_rows, wide), F32),
            pltpu.VMEM((out_rows, wide), BF16),
            pltpu.VMEM((out_rows, wide), BF16),
            pltpu.VMEM((n_cells * n_col, cell_rows, cell_cols), BF16),
            pltpu.VMEM((n_slots, LANES), jnp.int32),
            pltpu.VMEM((len(AROUND), n_slots, LANES), jnp.int32),
            pltpu.SMEM((len(AROUND), n_slots, LANES), jnp.int32),
            dma((len(AROUND),)),
            dma((len(AROUND),)),
            dma((len(AROUND),)),
            dma((len(AROUND),)),
            dma((2 * n_col,)),
            dma((2 * n_col,)),
            dma,
        ],
        compiler_params=pltpu.CompilerParams(
            collective_id=0, has_side_effects=True, vmem_limit_bytes=48 * 2**20
        ),
    )(*args)


def solution(mesh):
    placed = (
        P(("frames", "row"), "col"),
        P(),
        P(),
        P(),
        P("col", None, None),
        P(("frames", "row"), "col", None),
        P(("frames", "row"), "col", None),
        P(("frames", "row"), "col"),
    )
    return jax.shard_map(
        functools.partial(on_device, mesh.shape["row"], mesh.shape["col"]),
        mesh=mesh,
        in_specs=placed,
        out_specs=P(("frames", "row"), "col"),
        check_vma=False,
    )
```

```python
import functools
import math

import jax
import jax.numpy as jnp
from jax import lax
from jax.experimental import pallas as pl
from jax.experimental.pallas import tpu as pltpu
from jax.sharding import PartitionSpec as P

BLUR = 8
SIGMA = 4.0
GAUSS_SUM = sum(math.exp(-(t * t) / (2.0 * SIGMA * SIGMA)) for t in range(-BLUR, BLUR + 1))
MESH = pl.DeviceIdType.MESH
F32 = jnp.float32
BF16 = jnp.bfloat16
LANES = 128
AROUND = [(i, j) for i in (-1, 0, 1) for j in (-1, 0, 1)]
HERE = 4
RIM_ROWS = 32


def gauss_band(shape, in_dim):
    step = lax.broadcasted_iota(jnp.int32, shape, in_dim) - lax.broadcasted_iota(
        jnp.int32, shape, 1 - in_dim
    )
    lag = step.astype(F32) - BLUR
    value = jnp.exp(-lag * lag / (2.0 * SIGMA * SIGMA)) * (1.0 / GAUSS_SUM)
    value = jnp.where((step >= 0) & (step <= 2 * BLUR), value, 0.0)
    high = value.astype(BF16)
    return high, (value - high.astype(F32)).astype(BF16)


def dot(a, b):
    return jnp.dot(a, b, preferred_element_type=F32)


def kernel(
    half,
    n_row,
    n_col,
    mask_hbm,
    across_hbm,
    down_hbm,
    weights_ref,
    library_ref,
    ids_ref,
    slots_ref,
    count_ref,
    out_ref,
    own,
    up_down,
    left_right,
    corners,
    mask_ext,
    tap_rows,
    down_mats,
    across_mats,
    first,
    total,
    high,
    low,
    cells,
    table,
    tables,
    tables_s,
    mask_send,
    mask_recv,
    table_send,
    table_recv,
    cell_send,
    cell_recv,
    table_sem,
    mask_ref,
    across_ref,
    down_ref,
    fetch_sems,
    pass_send,
    pass_recv,
):
    fetches = [
        pltpu.make_async_copy(source, target, fetch_sems.at[i])
        for i, (source, target) in enumerate(
            ((mask_hbm, mask_ref), (down_hbm, down_ref), (across_hbm, across_ref))
        )
    ]
    for fetch in fetches:
        fetch.start()
    rows, cols = mask_ref.shape
    kernels = across_ref.shape[0]
    taps = 2 * half + 1
    rim = half + BLUR
    wide = own.shape[1]
    out_rows = rows + 2 * BLUR
    blocks = cols // LANES
    n_cells, cell_rows, _ = library_ref.shape
    slot_rows = rows // cell_rows
    row, col = lax.axis_index("row"), lax.axis_index("col")

    def exists(dr, dc):
        ok = None
        for here, step, count in ((row, dr, n_row), (col, dc, n_col)):
            if step < 0:
                one = here >= -step
            elif step > 0:
                one = here < count - step
            else:
                continue
            ok = one if ok is None else ok & one
        return ok

    def device(dr, dc):
        return {"row": row + dr, "col": col + dc}

    peers = [(0, j) for j in range(-(n_col - 1), n_col) if j != 0]
    near = [o for o in AROUND if o != (0, 0)]
    partners = near + [o for o in peers if abs(o[1]) > 1]

    barrier = pltpu.get_barrier_semaphore()
    for o in partners:

        @pl.when(exists(*o))
        def _():
            pl.semaphore_signal(barrier, inc=1, device_id=device(*o), device_id_type=MESH)

    fetches[0].wait()
    pixels = mask_ref[...].astype(F32)
    pixels = jnp.concatenate([pixels, jnp.zeros((rows, wide - cols), F32)], axis=1)
    own[...] = pltpu.roll(pixels, rim, 1).astype(BF16)
    entries = ids_ref.shape[-1]
    at_slot = lax.broadcasted_iota(jnp.int32, table.shape, 0)
    value = jnp.zeros(table.shape, jnp.int32)
    for n in range(entries):
        entry = jnp.where(n < count_ref[0, 0], ids_ref[0, 0, n] + 1, 0)
        value = value + jnp.where(at_slot == slots_ref[0, 0, n], entry, 0)
    table[...] = value

    pl.semaphore_wait(barrier, sum(jnp.where(exists(*o), 1, 0) for o in partners))

    def mask_copy(dr, dc):
        row_part = {-1: pl.ds(0, RIM_ROWS), 0: pl.ds(0, rows), 1: pl.ds(rows - RIM_ROWS, RIM_ROWS)}
        col_part = {-1: pl.ds(0, LANES), 0: pl.ds(0, wide), 1: pl.ds(cols, LANES)}
        slot = AROUND.index((-dr, -dc))
        if dc == 0:
            target = up_down.at[(1 - dr) // 2]
        elif dr == 0:
            target = left_right.at[(1 - dc) // 2]
        else:
            target = corners.at[(1 - dr) // 2 * 2 + (1 - dc) // 2]
        return pltpu.make_async_remote_copy(
            src_ref=own.at[row_part[dr], col_part[dc]],
            dst_ref=target,
            send_sem=mask_send.at[slot],
            recv_sem=mask_recv.at[slot],
            device_id=device(dr, dc),
            device_id_type=MESH,
        )

    def table_copy(dr, dc):
        slot = AROUND.index((-dr, -dc))
        return pltpu.make_async_remote_copy(
            src_ref=table,
            dst_ref=tables.at[slot],
            send_sem=table_send.at[slot],
            recv_sem=table_recv.at[slot],
            device_id=device(dr, dc),
            device_id_type=MESH,
        )

    core = lax.rem(row, 2)
    half_cells = n_cells // 2

    def pass_on(dc, part):
        block = cells.at[pl.ds((col + dc) * n_cells + part * half_cells, half_cells)]
        return pltpu.make_async_remote_copy(
            src_ref=block,
            dst_ref=block,
            send_sem=pass_send.at[dc + n_col],
            recv_sem=pass_recv.at[dc + n_col],
            device_id=device(1 - 2 * core, 0),
            device_id_type=MESH,
        )

    def cell_copy(dc, owner):
        return pltpu.make_async_remote_copy(
            src_ref=library_ref.at[pl.ds(core * half_cells, half_cells)],
            dst_ref=cells.at[pl.ds(owner * n_cells + core * half_cells, half_cells)],
            send_sem=cell_send.at[dc + n_col],
            recv_sem=cell_recv.at[dc + n_col],
            device_id=device(0, dc),
            device_id_type=MESH,
        )

    for o in near:

        @pl.when(exists(*o))
        def _():
            mask_copy(*o).start()

    for o in near:

        @pl.when(exists(*o))
        def _():
            table_copy(*o).start()

    for _, dc in sorted(peers, key=lambda o: abs(o[1])):

        @pl.when(exists(0, dc))
        def _():
            cell_copy(dc, col).start()

    own_cells = pltpu.make_async_copy(
        library_ref, cells.at[pl.ds(col * n_cells, n_cells)], fetch_sems.at[3]
    )
    own_cells.start()

    fetches[1].wait()
    fetches[2].wait()
    tap_rows[...] = jnp.zeros_like(tap_rows)
    for k in range(kernels):
        tap_rows[0, 2 * k : 2 * k + 2, :taps] = down_ref[k].astype(F32)
        tap_rows[1, 2 * k : 2 * k + 2, :taps] = across_ref[k].astype(F32)
    pick = lax.broadcasted_iota(jnp.int32, (LANES, 2 * LANES), 0)
    lane = lax.broadcasted_iota(jnp.int32, (LANES, 2 * LANES), 1)
    shift = RIM_ROWS - rim
    forward = (lane == pick + shift).astype(BF16)
    backward = ((lane + pick) % (2 * LANES) == 0).astype(BF16)
    base_down = dot(tap_rows[0, :, :LANES].astype(BF16), forward)
    base_across = dot(tap_rows[1, :, :LANES].astype(BF16), backward)
    tap_rows[0] = base_down
    tap_rows[1] = base_across
    band_rows = down_mats.shape[1]

    def build(i, carry):
        one = jnp.broadcast_to(tap_rows[0, pl.ds(i, 1), :], (band_rows, 2 * LANES))
        down_mats[i] = pltpu.roll(one, 0, 1, stride=1, stride_axis=0).astype(BF16)
        one = jnp.broadcast_to(tap_rows[1, pl.ds(i, 1), :], (2 * LANES, 2 * LANES))
        across_mats[i] = pltpu.roll(one, 0, 1, stride=1, stride_axis=0).astype(BF16)
        return carry

    lax.fori_loop(0, 2 * kernels, build, 0)

    total[...] = jnp.zeros_like(total)
    mask_ext[rows + 2 * RIM_ROWS :, :] = jnp.zeros_like(mask_ext[rows + 2 * RIM_ROWS :, :])
    own_cells.wait()
    tables[HERE] = table[...]

    for o in near:
        slot = AROUND.index(o)

        @pl.when(exists(*o))
        def _():
            table_copy(-o[0], -o[1]).wait_recv()

        @pl.when(jnp.logical_not(exists(*o)))
        def _():
            tables[slot] = jnp.zeros(tables.shape[1:], jnp.int32)

    to_scalar = pltpu.make_async_copy(tables, tables_s, table_sem)
    to_scalar.start()

    for o in near:
        dr, dc = o

        @pl.when(exists(*o))
        def _():
            mask_copy(-dr, -dc).wait_recv()

        @pl.when(jnp.logical_not(exists(*o)))
        def _():
            if dc == 0:
                up_down[(1 + dr) // 2] = jnp.zeros(up_down.shape[1:], BF16)
            elif dr == 0:
                left_right[(1 + dc) // 2] = jnp.zeros(left_right.shape[1:], BF16)
            else:
                corners[(1 + dr) // 2 * 2 + (1 + dc) // 2] = jnp.zeros(corners.shape[1:], BF16)

    def extend(start, body, left, right):
        count = body.shape[0]
        part = pl.ds(start, count)
        near_edge = lax.broadcasted_iota(jnp.int32, (count, LANES), 1) < 2 * rim
        mask_ext[part, 0:LANES] = body[:, 0:LANES] + left
        mask_ext[part, LANES:cols] = body[:, LANES:cols]
        mask_ext[part, cols:wide] = body[:, cols:wide] + jnp.where(
            near_edge, right.astype(F32), 0.0
        ).astype(BF16)

    extend(0, up_down[0], corners[0], corners[1])
    extend(RIM_ROWS, own[...], left_right[0], left_right[1])
    extend(RIM_ROWS + rows, up_down[1], corners[2], corners[3])

    rest = out_rows - band_rows

    def down_pass(k, carry):
        lhs = down_mats[pl.ds(2 * k, 2)].reshape(2 * band_rows, 2 * LANES)
        got = dot(lhs, mask_ext[0 : 2 * LANES, :]).astype(BF16)
        first[2 * k, 0:band_rows] = got[:band_rows]
        first[2 * k + 1, 0:band_rows] = got[band_rows:]
        got = dot(lhs, mask_ext[band_rows : band_rows + 2 * LANES, :]).astype(BF16)
        first[2 * k, band_rows:] = got[:rest]
        first[2 * k + 1, band_rows:] = got[band_rows : band_rows + rest]
        return carry

    lax.fori_loop(0, kernels, down_pass, 0)

    for _, dc in peers:

        @pl.when(exists(0, dc))
        def _():
            cell_copy(-dc, col + dc).wait_recv()
            pass_on(dc, core).start()

    def across_pass(k, carry):
        weight = weights_ref[k]
        for w in range(blocks):
            start = w * LANES
            stop = start + LANES if w < blocks - 1 else wide
            sums = None
            for p in range(2):
                got = dot(
                    first[2 * k + p, :, start : start + 2 * LANES],
                    across_mats[2 * k + p, :, : stop - start],
                )
                sums = got * got if sums is None else sums + got * got
            total[:, start:stop] = total[:, start:stop] + weight * sums
        return carry

    lax.fori_loop(0, kernels, across_pass, 0)

    for _, dc in peers:

        @pl.when(exists(0, dc))
        def _():
            pass_on(dc, 1 - core).wait_recv()

    to_scalar.wait()

    def image(where, slot, part):
        entry = tables_s[where, slot, 0]
        scale = jnp.where(entry > 0, 1.0, 0.0)
        index = jnp.minimum(jnp.maximum(entry - 1, 0), cells.shape[0] - 1)
        return cells[index, part, :].astype(F32) * scale

    def place(start, dr, slot_row, part, keep):
        middle = AROUND.index((dr, 0))
        pieces = [image(middle, slot_row * blocks + b, part) for b in range(blocks)]
        before = image(middle - 1, slot_row * blocks + blocks - 1, part)
        after = image(middle + 1, slot_row * blocks, part)
        first_half = lax.broadcasted_iota(jnp.int32, before.shape, 1) < LANES // 2
        pieces.append(jnp.where(first_half, after, before))
        band = pltpu.roll(jnp.concatenate(pieces, axis=1), BLUR, 1)[keep]
        total[start : start + band.shape[0], :] = total[start : start + band.shape[0], :] + band

    place(0, -1, slot_rows - 1, pl.ds(cell_rows - 16, 16), slice(8, 16))
    for a in range(slot_rows):
        place(BLUR + a * cell_rows, 0, a, pl.ds(0, cell_rows), slice(0, cell_rows))
    place(BLUR + rows, 1, 0, pl.ds(0, 16), slice(0, 8))

    row_from = jnp.where(row == 0, BLUR, 0)
    row_to = jnp.where(row == n_row - 1, BLUR + rows, out_rows)
    col_from = jnp.where(col == 0, BLUR, 0)
    col_to = jnp.where(col == n_col - 1, BLUR + cols, cols + 2 * BLUR)
    at_row = lax.broadcasted_iota(jnp.int32, (out_rows, wide), 0)
    at_col = lax.broadcasted_iota(jnp.int32, (out_rows, wide), 1)
    inside = (at_row >= row_from) & (at_row < row_to) & (at_col >= col_from) & (at_col < col_to)
    value = jnp.where(inside, total[...], 0.0)
    top = value.astype(BF16)
    high[...] = top
    low[...] = (value - top.astype(F32)).astype(BF16)

    g_high, g_low = gauss_band((2 * LANES, LANES), 0)
    for w in range(blocks):
        here = slice(w * LANES, (w + 2) * LANES)
        got = dot(high[:, here], g_high) + dot(low[:, here], g_high) + dot(high[:, here], g_low)
        total[:, w * LANES : (w + 1) * LANES] = got
    value = total[:, :cols]
    top = value.astype(BF16)
    high[:, :cols] = top
    low[:, :cols] = (value - top.astype(F32)).astype(BF16)
    g_high, g_low = gauss_band((LANES, LANES + 2 * BLUR), 1)
    for r in range(rows // LANES):
        here = slice(r * LANES, (r + 1) * LANES + 2 * BLUR)
        out_ref[r * LANES : (r + 1) * LANES, :] = (
            dot(g_high, high[here, :cols])
            + dot(g_high, low[here, :cols])
            + dot(g_low, high[here, :cols])
        )

    for o in near:

        @pl.when(exists(*o))
        def _():
            mask_copy(*o).wait_send()
            table_copy(*o).wait_send()

    for _, dc in peers:

        @pl.when(exists(0, dc))
        def _():
            cell_copy(dc, col).wait_send()
            pass_on(dc, core).wait_send()


def on_device(n_row, n_col, *args):
    mask_pixels, across_taps, _, _, library, cell_ids, _, _ = args
    rows, cols = mask_pixels.shape
    kernels = across_taps.shape[0]
    half = (across_taps.shape[-1] - 1) // 2
    wide = cols + LANES
    out_rows = rows + 2 * BLUR
    n_cells, cell_rows, cell_cols = library.shape
    n_slots = (rows // cell_rows) * (cols // cell_cols)
    band_rows = 144
    vmem = pl.BlockSpec(memory_space=pltpu.VMEM)
    hbm = pl.BlockSpec(memory_space=pltpu.HBM)
    smem = pl.BlockSpec(memory_space=pltpu.SMEM)
    dma = pltpu.SemaphoreType.DMA
    return pl.pallas_call(
        functools.partial(kernel, half, n_row, n_col),
        out_shape=jax.ShapeDtypeStruct((rows, cols), F32),
        in_specs=[hbm, hbm, hbm, smem, hbm, smem, smem, smem],
        out_specs=vmem,
        scratch_shapes=[
            pltpu.VMEM((rows, wide), BF16),
            pltpu.VMEM((2, RIM_ROWS, wide), BF16),
            pltpu.VMEM((2, rows, LANES), BF16),
            pltpu.VMEM((4, RIM_ROWS, LANES), BF16),
            pltpu.VMEM((band_rows + 2 * LANES, wide), BF16),
            pltpu.VMEM((2, 2 * kernels, 2 * LANES), F32),
            pltpu.VMEM((2 * kernels, band_rows, 2 * LANES), BF16),
            pltpu.VMEM((2 * kernels, 2 * LANES, 2 * LANES), BF16),
            pltpu.VMEM((2 * kernels, out_rows, wide), BF16),
            pltpu.VMEM((out_rows, wide), F32),
            pltpu.VMEM((out_rows, wide), BF16),
            pltpu.VMEM((out_rows, wide), BF16),
            pltpu.VMEM((n_cells * n_col, cell_rows, cell_cols), BF16),
            pltpu.VMEM((n_slots, LANES), jnp.int32),
            pltpu.VMEM((len(AROUND), n_slots, LANES), jnp.int32),
            pltpu.SMEM((len(AROUND), n_slots, LANES), jnp.int32),
            dma((len(AROUND),)),
            dma((len(AROUND),)),
            dma((len(AROUND),)),
            dma((len(AROUND),)),
            dma((2 * n_col,)),
            dma((2 * n_col,)),
            dma,
            pltpu.VMEM(mask_pixels.shape, mask_pixels.dtype),
            pltpu.VMEM(across_taps.shape, across_taps.dtype),
            pltpu.VMEM(across_taps.shape, across_taps.dtype),
            dma((4,)),
            dma((2 * n_col,)),
            dma((2 * n_col,)),
        ],
        compiler_params=pltpu.CompilerParams(
            collective_id=0, has_side_effects=True, vmem_limit_bytes=62 * 2**20
        ),
    )(*args)


def solution(mesh):
    placed = (
        P(("frames", "row"), "col"),
        P(),
        P(),
        P(),
        P("col", None, None),
        P(("frames", "row"), "col", None),
        P(("frames", "row"), "col", None),
        P(("frames", "row"), "col"),
    )
    return jax.shard_map(
        functools.partial(on_device, mesh.shape["row"], mesh.shape["col"]),
        mesh=mesh,
        in_specs=placed,
        out_specs=P(("frames", "row"), "col"),
        check_vma=False,
    )
```

```python
import functools
import math

import jax
import jax.numpy as jnp
from jax import lax
from jax.experimental import pallas as pl
from jax.experimental.pallas import tpu as pltpu
from jax.sharding import PartitionSpec as P

BLUR = 8
SIGMA = 4.0
GAUSS_SUM = sum(math.exp(-(t * t) / (2.0 * SIGMA * SIGMA)) for t in range(-BLUR, BLUR + 1))
MESH = pl.DeviceIdType.MESH
F32 = jnp.float32
BF16 = jnp.bfloat16
LANES = 128
AROUND = [(i, j) for i in (-1, 0, 1) for j in (-1, 0, 1)]
HERE = 4
RIM_ROWS = 32


def gauss_band(shape, in_dim):
    step = lax.broadcasted_iota(jnp.int32, shape, in_dim) - lax.broadcasted_iota(
        jnp.int32, shape, 1 - in_dim
    )
    lag = step.astype(F32) - BLUR
    value = jnp.exp(-lag * lag / (2.0 * SIGMA * SIGMA)) * (1.0 / GAUSS_SUM)
    value = jnp.where((step >= 0) & (step <= 2 * BLUR), value, 0.0)
    high = value.astype(BF16)
    return high, (value - high.astype(F32)).astype(BF16)


def dot(a, b):
    return jnp.dot(a, b, preferred_element_type=F32)


def kernel(
    half,
    n_row,
    n_col,
    mask_hbm,
    across_hbm,
    down_hbm,
    weights_ref,
    library_ref,
    ids_ref,
    slots_ref,
    count_ref,
    out_ref,
    own,
    up_down,
    left_right,
    corners,
    mask_ext,
    tap_rows,
    down_mats,
    across_mats,
    first,
    total,
    high,
    low,
    cells,
    table,
    tables,
    tables_s,
    mask_send,
    mask_recv,
    table_send,
    table_recv,
    cell_send,
    cell_recv,
    table_sem,
    mask_ref,
    across_ref,
    down_ref,
    fetch_sems,
    pass_send,
    pass_recv,
):
    fetches = [
        pltpu.make_async_copy(source, target, fetch_sems.at[i])
        for i, (source, target) in enumerate(
            ((mask_hbm, mask_ref), (down_hbm, down_ref), (across_hbm, across_ref))
        )
    ]
    for fetch in fetches:
        fetch.start()
    rows, cols = mask_ref.shape
    kernels = across_ref.shape[0]
    taps = 2 * half + 1
    rim = half + BLUR
    wide = own.shape[1]
    out_rows = rows + 2 * BLUR
    blocks = cols // LANES
    n_cells, cell_rows, _ = library_ref.shape
    slot_rows = rows // cell_rows
    row, col = lax.axis_index("row"), lax.axis_index("col")

    def exists(dr, dc):
        ok = None
        for here, step, count in ((row, dr, n_row), (col, dc, n_col)):
            if step < 0:
                one = here >= -step
            elif step > 0:
                one = here < count - step
            else:
                continue
            ok = one if ok is None else ok & one
        return ok

    def device(dr, dc):
        return {"row": row + dr, "col": col + dc}

    peers = [(0, j) for j in range(-(n_col - 1), n_col) if j != 0]
    near = [o for o in AROUND if o != (0, 0)]
    partners = near + [o for o in peers if abs(o[1]) > 1]

    barrier = pltpu.get_barrier_semaphore()
    for o in partners:

        @pl.when(exists(*o))
        def _():
            pl.semaphore_signal(barrier, inc=1, device_id=device(*o), device_id_type=MESH)

    fetches[0].wait()
    pixels = mask_ref[...].astype(F32)
    pixels = jnp.concatenate([pixels, jnp.zeros((rows, wide - cols), F32)], axis=1)
    own[...] = pltpu.roll(pixels, rim, 1).astype(BF16)
    entries = ids_ref.shape[-1]
    at_slot = lax.broadcasted_iota(jnp.int32, table.shape, 0)
    value = jnp.zeros(table.shape, jnp.int32)
    for n in range(entries):
        entry = jnp.where(n < count_ref[0, 0], ids_ref[0, 0, n] + 1, 0)
        value = value + jnp.where(at_slot == slots_ref[0, 0, n], entry, 0)
    table[...] = value

    pl.semaphore_wait(barrier, sum(jnp.where(exists(*o), 1, 0) for o in partners))

    def mask_copy(dr, dc):
        row_part = {-1: pl.ds(0, RIM_ROWS), 0: pl.ds(0, rows), 1: pl.ds(rows - RIM_ROWS, RIM_ROWS)}
        col_part = {-1: pl.ds(0, LANES), 0: pl.ds(0, wide), 1: pl.ds(cols, LANES)}
        slot = AROUND.index((-dr, -dc))
        if dc == 0:
            target = up_down.at[(1 - dr) // 2]
        elif dr == 0:
            target = left_right.at[(1 - dc) // 2]
        else:
            target = corners.at[(1 - dr) // 2 * 2 + (1 - dc) // 2]
        return pltpu.make_async_remote_copy(
            src_ref=own.at[row_part[dr], col_part[dc]],
            dst_ref=target,
            send_sem=mask_send.at[slot],
            recv_sem=mask_recv.at[slot],
            device_id=device(dr, dc),
            device_id_type=MESH,
        )

    def table_copy(dr, dc):
        slot = AROUND.index((-dr, -dc))
        return pltpu.make_async_remote_copy(
            src_ref=table,
            dst_ref=tables.at[slot],
            send_sem=table_send.at[slot],
            recv_sem=table_recv.at[slot],
            device_id=device(dr, dc),
            device_id_type=MESH,
        )

    core = lax.rem(row, 2)
    half_cells = n_cells // 2

    def pass_on(dc, part):
        block = cells.at[pl.ds((col + dc) * n_cells + part * half_cells, half_cells)]
        return pltpu.make_async_remote_copy(
            src_ref=block,
            dst_ref=block,
            send_sem=pass_send.at[dc + n_col],
            recv_sem=pass_recv.at[dc + n_col],
            device_id=device(1 - 2 * core, 0),
            device_id_type=MESH,
        )

    def cell_copy(dc, owner):
        return pltpu.make_async_remote_copy(
            src_ref=library_ref.at[pl.ds(core * half_cells, half_cells)],
            dst_ref=cells.at[pl.ds(owner * n_cells + core * half_cells, half_cells)],
            send_sem=cell_send.at[dc + n_col],
            recv_sem=cell_recv.at[dc + n_col],
            device_id=device(0, dc),
            device_id_type=MESH,
        )

    for o in near:

        @pl.when(exists(*o))
        def _():
            mask_copy(*o).start()

    for o in near:

        @pl.when(exists(*o))
        def _():
            table_copy(*o).start()

    for _, dc in sorted(peers, key=lambda o: abs(o[1])):

        @pl.when(exists(0, dc))
        def _():
            cell_copy(dc, col).start()

    own_cells = pltpu.make_async_copy(
        library_ref, cells.at[pl.ds(col * n_cells, n_cells)], fetch_sems.at[3]
    )
    own_cells.start()

    fetches[1].wait()
    fetches[2].wait()
    tap_rows[...] = jnp.zeros_like(tap_rows)
    for k in range(kernels):
        tap_rows[0, 2 * k : 2 * k + 2, :taps] = down_ref[k].astype(F32)
        tap_rows[1, 2 * k : 2 * k + 2, :taps] = across_ref[k].astype(F32)
    pick = lax.broadcasted_iota(jnp.int32, (LANES, 2 * LANES), 0)
    lane = lax.broadcasted_iota(jnp.int32, (LANES, 2 * LANES), 1)
    shift = RIM_ROWS - rim
    forward = (lane == pick + shift).astype(BF16)
    backward = ((lane + pick) % (2 * LANES) == 0).astype(BF16)
    base_down = dot(tap_rows[0, :, :LANES].astype(BF16), forward)
    base_across = dot(tap_rows[1, :, :LANES].astype(BF16), backward)
    tap_rows[0] = base_down
    tap_rows[1] = base_across
    band_rows = down_mats.shape[1]

    def build(i, carry):
        one = jnp.broadcast_to(tap_rows[0, pl.ds(i, 1), :], (band_rows, 2 * LANES))
        down_mats[i] = pltpu.roll(one, 0, 1, stride=1, stride_axis=0).astype(BF16)
        one = jnp.broadcast_to(tap_rows[1, pl.ds(i, 1), :], (2 * LANES, 2 * LANES))
        across_mats[i] = pltpu.roll(one, 0, 1, stride=1, stride_axis=0).astype(BF16)
        return carry

    lax.fori_loop(0, 2 * kernels, build, 0, unroll=4)

    total[...] = jnp.zeros_like(total)
    mask_ext[rows + 2 * RIM_ROWS :, :] = jnp.zeros_like(mask_ext[rows + 2 * RIM_ROWS :, :])
    own_cells.wait()
    tables[HERE] = table[...]

    for o in near:
        slot = AROUND.index(o)

        @pl.when(exists(*o))
        def _():
            table_copy(-o[0], -o[1]).wait_recv()

        @pl.when(jnp.logical_not(exists(*o)))
        def _():
            tables[slot] = jnp.zeros(tables.shape[1:], jnp.int32)

    to_scalar = pltpu.make_async_copy(tables, tables_s, table_sem)
    to_scalar.start()

    for o in near:
        dr, dc = o

        @pl.when(exists(*o))
        def _():
            mask_copy(-dr, -dc).wait_recv()

        @pl.when(jnp.logical_not(exists(*o)))
        def _():
            if dc == 0:
                up_down[(1 + dr) // 2] = jnp.zeros(up_down.shape[1:], BF16)
            elif dr == 0:
                left_right[(1 + dc) // 2] = jnp.zeros(left_right.shape[1:], BF16)
            else:
                corners[(1 + dr) // 2 * 2 + (1 + dc) // 2] = jnp.zeros(corners.shape[1:], BF16)

    def extend(start, body, left, right):
        count = body.shape[0]
        part = pl.ds(start, count)
        near_edge = lax.broadcasted_iota(jnp.int32, (count, LANES), 1) < 2 * rim
        mask_ext[part, 0:LANES] = body[:, 0:LANES] + left
        mask_ext[part, LANES:cols] = body[:, LANES:cols]
        mask_ext[part, cols:wide] = body[:, cols:wide] + jnp.where(
            near_edge, right.astype(F32), 0.0
        ).astype(BF16)

    extend(0, up_down[0], corners[0], corners[1])
    extend(RIM_ROWS, own[...], left_right[0], left_right[1])
    extend(RIM_ROWS + rows, up_down[1], corners[2], corners[3])

    rest = out_rows - band_rows

    def down_pass(k, carry):
        lhs = down_mats[pl.ds(2 * k, 2)].reshape(2 * band_rows, 2 * LANES)
        got = dot(lhs, mask_ext[0 : 2 * LANES, :]).astype(BF16)
        first[2 * k, 0:band_rows] = got[:band_rows]
        first[2 * k + 1, 0:band_rows] = got[band_rows:]
        got = dot(lhs, mask_ext[band_rows : band_rows + 2 * LANES, :]).astype(BF16)
        first[2 * k, band_rows:] = got[:rest]
        first[2 * k + 1, band_rows:] = got[band_rows : band_rows + rest]
        return carry

    lax.fori_loop(0, kernels, down_pass, 0, unroll=2)

    for _, dc in peers:

        @pl.when(exists(0, dc))
        def _():
            cell_copy(-dc, col + dc).wait_recv()
            pass_on(dc, core).start()

    def across_pass(k, carry):
        weight = weights_ref[k]
        for w in range(blocks):
            start = w * LANES
            stop = start + LANES if w < blocks - 1 else wide
            sums = None
            for p in range(2):
                got = dot(
                    first[2 * k + p, :, start : start + 2 * LANES],
                    across_mats[2 * k + p, :, : stop - start],
                )
                sums = got * got if sums is None else sums + got * got
            total[:, start:stop] = total[:, start:stop] + weight * sums
        return carry

    lax.fori_loop(0, kernels, across_pass, 0, unroll=3)

    for _, dc in peers:

        @pl.when(exists(0, dc))
        def _():
            pass_on(dc, 1 - core).wait_recv()

    to_scalar.wait()

    def image(where, slot, part):
        entry = tables_s[where, slot, 0]
        scale = jnp.where(entry > 0, 1.0, 0.0)
        index = jnp.minimum(jnp.maximum(entry - 1, 0), cells.shape[0] - 1)
        return cells[index, part, :].astype(F32) * scale

    def place(start, dr, slot_row, part, keep):
        middle = AROUND.index((dr, 0))
        pieces = [image(middle, slot_row * blocks + b, part) for b in range(blocks)]
        before = image(middle - 1, slot_row * blocks + blocks - 1, part)
        after = image(middle + 1, slot_row * blocks, part)
        first_half = lax.broadcasted_iota(jnp.int32, before.shape, 1) < LANES // 2
        pieces.append(jnp.where(first_half, after, before))
        band = pltpu.roll(jnp.concatenate(pieces, axis=1), BLUR, 1)[keep]
        total[start : start + band.shape[0], :] = total[start : start + band.shape[0], :] + band

    place(0, -1, slot_rows - 1, pl.ds(cell_rows - 16, 16), slice(8, 16))
    for a in range(slot_rows):
        place(BLUR + a * cell_rows, 0, a, pl.ds(0, cell_rows), slice(0, cell_rows))
    place(BLUR + rows, 1, 0, pl.ds(0, 16), slice(0, 8))

    row_from = jnp.where(row == 0, BLUR, 0)
    row_to = jnp.where(row == n_row - 1, BLUR + rows, out_rows)
    col_from = jnp.where(col == 0, BLUR, 0)
    col_to = jnp.where(col == n_col - 1, BLUR + cols, cols + 2 * BLUR)
    at_row = lax.broadcasted_iota(jnp.int32, (out_rows, wide), 0)
    at_col = lax.broadcasted_iota(jnp.int32, (out_rows, wide), 1)
    inside = (at_row >= row_from) & (at_row < row_to) & (at_col >= col_from) & (at_col < col_to)
    value = jnp.where(inside, total[...], 0.0)
    top = value.astype(BF16)
    high[...] = top
    low[...] = (value - top.astype(F32)).astype(BF16)

    g_high, g_low = gauss_band((2 * LANES, LANES), 0)
    for w in range(blocks):
        here = slice(w * LANES, (w + 2) * LANES)
        got = dot(high[:, here], g_high) + dot(low[:, here], g_high) + dot(high[:, here], g_low)
        total[:, w * LANES : (w + 1) * LANES] = got
    value = total[:, :cols]
    top = value.astype(BF16)
    high[:, :cols] = top
    low[:, :cols] = (value - top.astype(F32)).astype(BF16)
    g_high, g_low = gauss_band((LANES, LANES + 2 * BLUR), 1)
    for r in range(rows // LANES):
        here = slice(r * LANES, (r + 1) * LANES + 2 * BLUR)
        out_ref[r * LANES : (r + 1) * LANES, :] = (
            dot(g_high, high[here, :cols])
            + dot(g_high, low[here, :cols])
            + dot(g_low, high[here, :cols])
        )

    for o in near:

        @pl.when(exists(*o))
        def _():
            mask_copy(*o).wait_send()
            table_copy(*o).wait_send()

    for _, dc in peers:

        @pl.when(exists(0, dc))
        def _():
            cell_copy(dc, col).wait_send()
            pass_on(dc, core).wait_send()


def on_device(n_row, n_col, *args):
    mask_pixels, across_taps, _, _, library, cell_ids, _, _ = args
    rows, cols = mask_pixels.shape
    kernels = across_taps.shape[0]
    half = (across_taps.shape[-1] - 1) // 2
    wide = cols + LANES
    out_rows = rows + 2 * BLUR
    n_cells, cell_rows, cell_cols = library.shape
    n_slots = (rows // cell_rows) * (cols // cell_cols)
    band_rows = 144
    vmem = pl.BlockSpec(memory_space=pltpu.VMEM)
    hbm = pl.BlockSpec(memory_space=pltpu.HBM)
    smem = pl.BlockSpec(memory_space=pltpu.SMEM)
    dma = pltpu.SemaphoreType.DMA
    return pl.pallas_call(
        functools.partial(kernel, half, n_row, n_col),
        out_shape=jax.ShapeDtypeStruct((rows, cols), F32),
        in_specs=[hbm, hbm, hbm, smem, hbm, smem, smem, smem],
        out_specs=vmem,
        scratch_shapes=[
            pltpu.VMEM((rows, wide), BF16),
            pltpu.VMEM((2, RIM_ROWS, wide), BF16),
            pltpu.VMEM((2, rows, LANES), BF16),
            pltpu.VMEM((4, RIM_ROWS, LANES), BF16),
            pltpu.VMEM((band_rows + 2 * LANES, wide), BF16),
            pltpu.VMEM((2, 2 * kernels, 2 * LANES), F32),
            pltpu.VMEM((2 * kernels, band_rows, 2 * LANES), BF16),
            pltpu.VMEM((2 * kernels, 2 * LANES, 2 * LANES), BF16),
            pltpu.VMEM((2 * kernels, out_rows, wide), BF16),
            pltpu.VMEM((out_rows, wide), F32),
            pltpu.VMEM((out_rows, wide), BF16),
            pltpu.VMEM((out_rows, wide), BF16),
            pltpu.VMEM((n_cells * n_col, cell_rows, cell_cols), BF16),
            pltpu.VMEM((n_slots, LANES), jnp.int32),
            pltpu.VMEM((len(AROUND), n_slots, LANES), jnp.int32),
            pltpu.SMEM((len(AROUND), n_slots, LANES), jnp.int32),
            dma((len(AROUND),)),
            dma((len(AROUND),)),
            dma((len(AROUND),)),
            dma((len(AROUND),)),
            dma((2 * n_col,)),
            dma((2 * n_col,)),
            dma,
            pltpu.VMEM(mask_pixels.shape, mask_pixels.dtype),
            pltpu.VMEM(across_taps.shape, across_taps.dtype),
            pltpu.VMEM(across_taps.shape, across_taps.dtype),
            dma((4,)),
            dma((2 * n_col,)),
            dma((2 * n_col,)),
        ],
        compiler_params=pltpu.CompilerParams(
            collective_id=0, has_side_effects=True, vmem_limit_bytes=62 * 2**20
        ),
    )(*args)


def solution(mesh):
    placed = (
        P(("frames", "row"), "col"),
        P(),
        P(),
        P(),
        P("col", None, None),
        P(("frames", "row"), "col", None),
        P(("frames", "row"), "col", None),
        P(("frames", "row"), "col"),
    )
    return jax.shard_map(
        functools.partial(on_device, mesh.shape["row"], mesh.shape["col"]),
        mesh=mesh,
        in_specs=placed,
        out_specs=P(("frames", "row"), "col"),
        check_vma=False,
    )
```

```python
import functools
import math

import jax
import jax.numpy as jnp
from jax import lax
from jax.experimental import pallas as pl
from jax.experimental.pallas import tpu as pltpu
from jax.sharding import PartitionSpec as P

BLUR = 8
SIGMA = 4.0
GAUSS_SUM = sum(math.exp(-(t * t) / (2.0 * SIGMA * SIGMA)) for t in range(-BLUR, BLUR + 1))
MESH = pl.DeviceIdType.MESH
F32 = jnp.float32
BF16 = jnp.bfloat16
LANES = 128
AROUND = [(i, j) for i in (-1, 0, 1) for j in (-1, 0, 1)]
HERE = 4
RIM_ROWS = 32


def gauss_band(shape, in_dim):
    step = lax.broadcasted_iota(jnp.int32, shape, in_dim) - lax.broadcasted_iota(
        jnp.int32, shape, 1 - in_dim
    )
    lag = step.astype(F32) - BLUR
    value = jnp.exp(-lag * lag / (2.0 * SIGMA * SIGMA)) * (1.0 / GAUSS_SUM)
    value = jnp.where((step >= 0) & (step <= 2 * BLUR), value, 0.0)
    high = value.astype(BF16)
    return high, (value - high.astype(F32)).astype(BF16)


def dot(a, b):
    return jnp.dot(a, b, preferred_element_type=F32)


def kernel(
    half,
    n_row,
    n_col,
    mask_hbm,
    across_hbm,
    down_hbm,
    weights_ref,
    library_ref,
    ids_ref,
    slots_ref,
    count_ref,
    out_ref,
    own,
    up_down,
    left_right,
    corners,
    mask_ext,
    tap_rows,
    down_mats,
    across_mats,
    first,
    total,
    high,
    low,
    cells,
    table,
    tables,
    tables_s,
    mask_send,
    mask_recv,
    table_send,
    table_recv,
    cell_send,
    cell_recv,
    table_sem,
    mask_ref,
    across_ref,
    down_ref,
    fetch_sems,
    pass_send,
    pass_recv,
):
    fetches = [
        pltpu.make_async_copy(source, target, fetch_sems.at[i])
        for i, (source, target) in enumerate(
            ((mask_hbm, mask_ref), (down_hbm, down_ref), (across_hbm, across_ref))
        )
    ]
    for fetch in fetches:
        fetch.start()
    rows, cols = mask_ref.shape
    kernels = across_ref.shape[0]
    taps = 2 * half + 1
    rim = half + BLUR
    wide = own.shape[1]
    out_rows = rows + 2 * BLUR
    blocks = cols // LANES
    n_cells, cell_rows, _ = library_ref.shape
    slot_rows = rows // cell_rows
    row, col = lax.axis_index("row"), lax.axis_index("col")

    def exists(dr, dc):
        ok = None
        for here, step, count in ((row, dr, n_row), (col, dc, n_col)):
            if step < 0:
                one = here >= -step
            elif step > 0:
                one = here < count - step
            else:
                continue
            ok = one if ok is None else ok & one
        return ok

    def device(dr, dc):
        return {"row": row + dr, "col": col + dc}

    peers = [(0, j) for j in range(-(n_col - 1), n_col) if j != 0]
    near = [o for o in AROUND if o != (0, 0)]
    partners = near + [o for o in peers if abs(o[1]) > 1]

    barrier = pltpu.get_barrier_semaphore()
    for o in partners:

        @pl.when(exists(*o))
        def _():
            pl.semaphore_signal(barrier, inc=1, device_id=device(*o), device_id_type=MESH)

    fetches[0].wait()
    pixels = mask_ref[...].astype(F32)
    pixels = jnp.concatenate([pixels, jnp.zeros((rows, wide - cols), F32)], axis=1)
    own[...] = pltpu.roll(pixels, rim, 1).astype(BF16)
    entries = ids_ref.shape[-1]
    at_slot = lax.broadcasted_iota(jnp.int32, table.shape, 0)
    value = jnp.zeros(table.shape, jnp.int32)
    for n in range(entries):
        entry = jnp.where(n < count_ref[0, 0], ids_ref[0, 0, n] + 1, 0)
        value = value + jnp.where(at_slot == slots_ref[0, 0, n], entry, 0)
    table[...] = value

    pl.semaphore_wait(barrier, sum(jnp.where(exists(*o), 1, 0) for o in partners))

    def mask_copy(dr, dc):
        row_part = {-1: pl.ds(0, RIM_ROWS), 0: pl.ds(0, rows), 1: pl.ds(rows - RIM_ROWS, RIM_ROWS)}
        col_part = {-1: pl.ds(0, LANES), 0: pl.ds(0, wide), 1: pl.ds(cols, LANES)}
        slot = AROUND.index((-dr, -dc))
        if dc == 0:
            target = up_down.at[(1 - dr) // 2]
        elif dr == 0:
            target = left_right.at[(1 - dc) // 2]
        else:
            target = corners.at[(1 - dr) // 2 * 2 + (1 - dc) // 2]
        return pltpu.make_async_remote_copy(
            src_ref=own.at[row_part[dr], col_part[dc]],
            dst_ref=target,
            send_sem=mask_send.at[slot],
            recv_sem=mask_recv.at[slot],
            device_id=device(dr, dc),
            device_id_type=MESH,
        )

    def table_copy(dr, dc):
        slot = AROUND.index((-dr, -dc))
        return pltpu.make_async_remote_copy(
            src_ref=table,
            dst_ref=tables.at[slot],
            send_sem=table_send.at[slot],
            recv_sem=table_recv.at[slot],
            device_id=device(dr, dc),
            device_id_type=MESH,
        )

    core = lax.rem(row, 2)
    half_cells = n_cells // 2

    def pass_on(dc, part):
        block = cells.at[pl.ds((col + dc) * n_cells + part * half_cells, half_cells)]
        return pltpu.make_async_remote_copy(
            src_ref=block,
            dst_ref=block,
            send_sem=pass_send.at[dc + n_col],
            recv_sem=pass_recv.at[dc + n_col],
            device_id=device(1 - 2 * core, 0),
            device_id_type=MESH,
        )

    def cell_copy(dc, owner):
        return pltpu.make_async_remote_copy(
            src_ref=library_ref.at[pl.ds(core * half_cells, half_cells)],
            dst_ref=cells.at[pl.ds(owner * n_cells + core * half_cells, half_cells)],
            send_sem=cell_send.at[dc + n_col],
            recv_sem=cell_recv.at[dc + n_col],
            device_id=device(0, dc),
            device_id_type=MESH,
        )

    for o in near:

        @pl.when(exists(*o))
        def _():
            mask_copy(*o).start()

    for o in near:

        @pl.when(exists(*o))
        def _():
            table_copy(*o).start()

    for _, dc in sorted(peers, key=lambda o: abs(o[1])):

        @pl.when(exists(0, dc))
        def _():
            cell_copy(dc, col).start()

    own_cells = pltpu.make_async_copy(
        library_ref, cells.at[pl.ds(col * n_cells, n_cells)], fetch_sems.at[3]
    )
    own_cells.start()

    fetches[1].wait()
    fetches[2].wait()
    tap_rows[...] = jnp.zeros_like(tap_rows)
    for k in range(kernels):
        tap_rows[0, 2 * k : 2 * k + 2, :taps] = down_ref[k].astype(F32)
        tap_rows[1, 2 * k : 2 * k + 2, :taps] = across_ref[k].astype(F32)
    pick = lax.broadcasted_iota(jnp.int32, (LANES, 2 * LANES), 0)
    lane = lax.broadcasted_iota(jnp.int32, (LANES, 2 * LANES), 1)
    shift = RIM_ROWS - rim
    forward = (lane == pick + shift).astype(BF16)
    backward = ((lane + pick) % (2 * LANES) == 0).astype(BF16)
    base_down = dot(tap_rows[0, :, :LANES].astype(BF16), forward)
    base_across = dot(tap_rows[1, :, :LANES].astype(BF16), backward)
    tap_rows[0] = base_down
    tap_rows[1] = base_across
    band_rows = down_mats.shape[1]

    def build(i, carry):
        one = jnp.broadcast_to(tap_rows[0, pl.ds(i, 1), :], (band_rows, 2 * LANES))
        down_mats[i] = pltpu.roll(one, 0, 1, stride=1, stride_axis=0).astype(BF16)
        one = jnp.broadcast_to(tap_rows[1, pl.ds(i, 1), :], (2 * LANES, 2 * LANES))
        across_mats[i] = pltpu.roll(one, 0, 1, stride=1, stride_axis=0).astype(BF16)
        return carry

    lax.fori_loop(0, 2 * kernels, build, 0, unroll=4)

    total[...] = jnp.zeros_like(total)
    mask_ext[rows + 2 * RIM_ROWS :, :] = jnp.zeros_like(mask_ext[rows + 2 * RIM_ROWS :, :])
    own_cells.wait()
    tables[HERE] = table[...]

    for o in near:
        slot = AROUND.index(o)

        @pl.when(exists(*o))
        def _():
            table_copy(-o[0], -o[1]).wait_recv()

        @pl.when(jnp.logical_not(exists(*o)))
        def _():
            tables[slot] = jnp.zeros(tables.shape[1:], jnp.int32)

    to_scalar = pltpu.make_async_copy(tables, tables_s, table_sem)
    to_scalar.start()

    for o in near:
        dr, dc = o

        @pl.when(exists(*o))
        def _():
            mask_copy(-dr, -dc).wait_recv()

        @pl.when(jnp.logical_not(exists(*o)))
        def _():
            if dc == 0:
                up_down[(1 + dr) // 2] = jnp.zeros(up_down.shape[1:], BF16)
            elif dr == 0:
                left_right[(1 + dc) // 2] = jnp.zeros(left_right.shape[1:], BF16)
            else:
                corners[(1 + dr) // 2 * 2 + (1 + dc) // 2] = jnp.zeros(corners.shape[1:], BF16)

    def extend(start, body, left, right):
        count = body.shape[0]
        part = pl.ds(start, count)
        near_edge = lax.broadcasted_iota(jnp.int32, (count, LANES), 1) < 2 * rim
        mask_ext[part, 0:LANES] = body[:, 0:LANES] + left
        mask_ext[part, LANES:cols] = body[:, LANES:cols]
        mask_ext[part, cols:wide] = body[:, cols:wide] + jnp.where(
            near_edge, right.astype(F32), 0.0
        ).astype(BF16)

    extend(0, up_down[0], corners[0], corners[1])
    extend(RIM_ROWS, own[...], left_right[0], left_right[1])
    extend(RIM_ROWS + rows, up_down[1], corners[2], corners[3])

    rest = out_rows - band_rows

    def down_pass(k, carry):
        lhs = down_mats[pl.ds(2 * k, 2)].reshape(2 * band_rows, 2 * LANES)
        got = dot(lhs, mask_ext[0 : 2 * LANES, :]).astype(BF16)
        first[2 * k, 0:band_rows] = got[:band_rows]
        first[2 * k + 1, 0:band_rows] = got[band_rows:]
        got = dot(lhs, mask_ext[band_rows : band_rows + 2 * LANES, :]).astype(BF16)
        first[2 * k, band_rows:] = got[:rest]
        first[2 * k + 1, band_rows:] = got[band_rows : band_rows + rest]
        return carry

    lax.fori_loop(0, kernels, down_pass, 0, unroll=2)

    def across_pass(k, carry):
        weight = weights_ref[k]
        for w in range(blocks):
            start = w * LANES
            stop = start + LANES if w < blocks - 1 else wide
            sums = None
            for p in range(2):
                got = dot(
                    first[2 * k + p, :, start : start + 2 * LANES],
                    across_mats[2 * k + p, :, : stop - start],
                )
                sums = got * got if sums is None else sums + got * got
            total[:, start:stop] = total[:, start:stop] + weight * sums
        return carry

    early = kernels * 3 // 4
    lax.fori_loop(0, early, across_pass, 0, unroll=3)

    for _, dc in peers:

        @pl.when(exists(0, dc))
        def _():
            cell_copy(-dc, col + dc).wait_recv()
            pass_on(dc, core).start()

    lax.fori_loop(early, kernels, across_pass, 0, unroll=3)

    for _, dc in peers:

        @pl.when(exists(0, dc))
        def _():
            pass_on(dc, 1 - core).wait_recv()

    to_scalar.wait()

    def image(where, slot, part):
        entry = tables_s[where, slot, 0]
        scale = jnp.where(entry > 0, 1.0, 0.0)
        index = jnp.minimum(jnp.maximum(entry - 1, 0), cells.shape[0] - 1)
        return cells[index, part, :].astype(F32) * scale

    def place(start, dr, slot_row, part, keep):
        middle = AROUND.index((dr, 0))
        pieces = [image(middle, slot_row * blocks + b, part) for b in range(blocks)]
        before = image(middle - 1, slot_row * blocks + blocks - 1, part)
        after = image(middle + 1, slot_row * blocks, part)
        first_half = lax.broadcasted_iota(jnp.int32, before.shape, 1) < LANES // 2
        pieces.append(jnp.where(first_half, after, before))
        band = pltpu.roll(jnp.concatenate(pieces, axis=1), BLUR, 1)[keep]
        total[start : start + band.shape[0], :] = total[start : start + band.shape[0], :] + band

    place(0, -1, slot_rows - 1, pl.ds(cell_rows - 16, 16), slice(8, 16))
    for a in range(slot_rows):
        place(BLUR + a * cell_rows, 0, a, pl.ds(0, cell_rows), slice(0, cell_rows))
    place(BLUR + rows, 1, 0, pl.ds(0, 16), slice(0, 8))

    row_from = jnp.where(row == 0, BLUR, 0)
    row_to = jnp.where(row == n_row - 1, BLUR + rows, out_rows)
    col_from = jnp.where(col == 0, BLUR, 0)
    col_to = jnp.where(col == n_col - 1, BLUR + cols, cols + 2 * BLUR)
    at_row = lax.broadcasted_iota(jnp.int32, (out_rows, wide), 0)
    at_col = lax.broadcasted_iota(jnp.int32, (out_rows, wide), 1)
    inside = (at_row >= row_from) & (at_row < row_to) & (at_col >= col_from) & (at_col < col_to)
    value = jnp.where(inside, total[...], 0.0)
    top = value.astype(BF16)
    high[...] = top
    low[...] = (value - top.astype(F32)).astype(BF16)

    g_high, g_low = gauss_band((2 * LANES, LANES), 0)
    for w in range(blocks):
        here = slice(w * LANES, (w + 2) * LANES)
        got = dot(high[:, here], g_high) + dot(low[:, here], g_high) + dot(high[:, here], g_low)
        total[:, w * LANES : (w + 1) * LANES] = got
    value = total[:, :cols]
    top = value.astype(BF16)
    high[:, :cols] = top
    low[:, :cols] = (value - top.astype(F32)).astype(BF16)
    g_high, g_low = gauss_band((LANES, LANES + 2 * BLUR), 1)
    for r in range(rows // LANES):
        here = slice(r * LANES, (r + 1) * LANES + 2 * BLUR)
        out_ref[r * LANES : (r + 1) * LANES, :] = (
            dot(g_high, high[here, :cols])
            + dot(g_high, low[here, :cols])
            + dot(g_low, high[here, :cols])
        )

    for o in near:

        @pl.when(exists(*o))
        def _():
            mask_copy(*o).wait_send()
            table_copy(*o).wait_send()

    for _, dc in peers:

        @pl.when(exists(0, dc))
        def _():
            cell_copy(dc, col).wait_send()
            pass_on(dc, core).wait_send()


def on_device(n_row, n_col, *args):
    mask_pixels, across_taps, _, _, library, cell_ids, _, _ = args
    rows, cols = mask_pixels.shape
    kernels = across_taps.shape[0]
    half = (across_taps.shape[-1] - 1) // 2
    wide = cols + LANES
    out_rows = rows + 2 * BLUR
    n_cells, cell_rows, cell_cols = library.shape
    n_slots = (rows // cell_rows) * (cols // cell_cols)
    band_rows = 144
    vmem = pl.BlockSpec(memory_space=pltpu.VMEM)
    hbm = pl.BlockSpec(memory_space=pltpu.HBM)
    smem = pl.BlockSpec(memory_space=pltpu.SMEM)
    dma = pltpu.SemaphoreType.DMA
    return pl.pallas_call(
        functools.partial(kernel, half, n_row, n_col),
        out_shape=jax.ShapeDtypeStruct((rows, cols), F32),
        in_specs=[hbm, hbm, hbm, smem, hbm, smem, smem, smem],
        out_specs=vmem,
        scratch_shapes=[
            pltpu.VMEM((rows, wide), BF16),
            pltpu.VMEM((2, RIM_ROWS, wide), BF16),
            pltpu.VMEM((2, rows, LANES), BF16),
            pltpu.VMEM((4, RIM_ROWS, LANES), BF16),
            pltpu.VMEM((band_rows + 2 * LANES, wide), BF16),
            pltpu.VMEM((2, 2 * kernels, 2 * LANES), F32),
            pltpu.VMEM((2 * kernels, band_rows, 2 * LANES), BF16),
            pltpu.VMEM((2 * kernels, 2 * LANES, 2 * LANES), BF16),
            pltpu.VMEM((2 * kernels, out_rows, wide), BF16),
            pltpu.VMEM((out_rows, wide), F32),
            pltpu.VMEM((out_rows, wide), BF16),
            pltpu.VMEM((out_rows, wide), BF16),
            pltpu.VMEM((n_cells * n_col, cell_rows, cell_cols), BF16),
            pltpu.VMEM((n_slots, LANES), jnp.int32),
            pltpu.VMEM((len(AROUND), n_slots, LANES), jnp.int32),
            pltpu.SMEM((len(AROUND), n_slots, LANES), jnp.int32),
            dma((len(AROUND),)),
            dma((len(AROUND),)),
            dma((len(AROUND),)),
            dma((len(AROUND),)),
            dma((2 * n_col,)),
            dma((2 * n_col,)),
            dma,
            pltpu.VMEM(mask_pixels.shape, mask_pixels.dtype),
            pltpu.VMEM(across_taps.shape, across_taps.dtype),
            pltpu.VMEM(across_taps.shape, across_taps.dtype),
            dma((4,)),
            dma((2 * n_col,)),
            dma((2 * n_col,)),
        ],
        compiler_params=pltpu.CompilerParams(
            collective_id=0, has_side_effects=True, vmem_limit_bytes=62 * 2**20
        ),
    )(*args)


def solution(mesh):
    placed = (
        P(("frames", "row"), "col"),
        P(),
        P(),
        P(),
        P("col", None, None),
        P(("frames", "row"), "col", None),
        P(("frames", "row"), "col", None),
        P(("frames", "row"), "col"),
    )
    return jax.shard_map(
        functools.partial(on_device, mesh.shape["row"], mesh.shape["col"]),
        mesh=mesh,
        in_specs=placed,
        out_specs=P(("frames", "row"), "col"),
        check_vma=False,
    )
```
